512 devices in a mesh: ctx: 32 (over y_lo, z, core), tp: 16 (over x, y_hi).
Axes of the slice: x: 4, y: 8 (y_hi: 4, y_lo: 2; y = y_hi * 2 + y_lo), z: 8, core: 2. Of those that a mesh axis runs over, the one named last changes fastest.
Arguments:
- projected: bfloat16 [3, 8192, 8192], P(None, 'ctx', 'tp'), may hold values from -6 to 6
- short_weight: float32 [3, 3, 8192], P(None, None, 'tp'), may hold values from -3.5 to 3.5
- filter_taps: float32 [8192, 8192], P(None, ('tp', 'ctx')), may hold values from -1.6 to 1.6, as said below
- out_weight: bfloat16 [8192, 8192], P('tp', 'ctx'), may hold values from -0.125 to 0.125
Outputs:
- block_out: bfloat16 [8192, 8192], P('ctx', 'tp')
The draws below stay inside these ranges and needn't reach their ends.
Inputs may be any that keep to these rules, and one draw needn't show every extreme that they name: `filter_taps`: taps of each channel's causal filter.
All inputs are finite; a program needn't handle non-finite values.
Results may differ from the reference program's by a relative error of at most 0.017.
Values may be sent and summed in bfloat16 or wider, within the bound.
No kernel may reach another device: no remote copies, remote signals or barrier semaphores. Data moves between devices by JAX's collectives and lax.ppermute only.
A program may use at most 64 MiB of HBM per device.

```python
import jax
import jax.numpy as jnp
from jax import lax

D = 8192
SHORT = 3
TOKENS = 8192
N_TP = 16


def draw_filter_taps(key, part):
    key = jax.random.fold_in(key, 11)
    key_slow, key_rate, key_noise = jax.random.split(key, 3)
    position = jnp.arange(TOKENS, dtype=jnp.float32)[:, None]
    slow_mask = jax.random.uniform(key_slow, (1, D)) < 0.5
    noise_part = jax.random.truncated_normal(key_noise, -6.0, 6.0, (TOKENS, D))
    fraction = jax.random.uniform(key_rate, (1, D))
    slow_rate = 0.2 / TOKENS * 10.0 ** fraction
    fast_rate = 2.0 / TOKENS * (TOKENS / 60.0) ** fraction
    decay_rate = jnp.where(slow_mask, slow_rate, fast_rate)
    return noise_part * jnp.exp(-decay_rate * position) * jnp.sqrt(2.0 * decay_rate)


def spiked(entries, own_key, source, target, parts, factor):
    def block_of(dim):
        return (jnp.arange(entries.shape[dim]) // (entries.shape[dim] // parts)).reshape((-1,) + (1,) * (entries.ndim - 1 - dim))

    near = jax.random.permutation(own_key, parts)[block_of(target)]
    second = (block_of(target) + parts // 2) % parts
    return jnp.where((block_of(source) == near) | (block_of(source) == second), factor * entries, entries)


def levels(stream_key, shape, shards, smallest, top_value):
    factor_of = 1.0
    for axis_at, shards_of in shards:
        steps = jax.random.uniform(jax.random.fold_in(jax.random.fold_in(stream_key, 6), axis_at), (shards_of,), jnp.float32, smallest / len(shards), top_value / len(shards))
        factor_of = factor_of * jnp.repeat(jnp.exp(steps), shape[axis_at] // shards_of).reshape((-1,) + (1,) * (len(shape) - 1 - axis_at))
    return factor_of


def centred(own_key, dims, spread, limit, cuts=(), kind=jnp.bfloat16):
    level = levels(own_key, dims, cuts, -0.22, 0.18) if cuts else 1.0
    entries = jax.random.normal(own_key, dims, jnp.float32) * spread * level
    return jnp.minimum(jnp.maximum(entries, -limit), limit).astype(kind)


def bell_draw_with(key, extent, width, reach, pieces, heavy, kind=jnp.bfloat16):
    entries = width * jax.random.normal(key, extent, jnp.float32)
    if pieces:
        entries = entries * levels(key, extent, pieces, -0.22, 0.18)
    return jnp.clip(spiked(entries, jax.random.fold_in(key, 3), *heavy), -reach, reach).astype(kind)


def setup_inputs(seed: int = 0) -> dict:
    key_of = jax.random.split(jax.random.key(seed), 5)
    projected = centred(key_of[0], (3, TOKENS, D), 1.0, 6.0, ((1, 32), (2, 16)))
    short_weight = centred(key_of[1], (3, SHORT, D), SHORT ** -0.5, 3.5, ((2, 16),), jnp.float32)
    filter_taps = draw_filter_taps(jax.random.fold_in(key_of[4], 71), 0)
    out_weight = bell_draw_with(key_of[3], (D, D), D ** -0.5, 0.125, ((0, 16), (1, 32)), (0, 1, 32, 2.75))
    return dict(projected=projected, short_weight=short_weight, filter_taps=filter_taps, out_weight=out_weight)


def short_filter(signal_in, tap_weights, lead_rows):
    row_count = signal_in.shape[1] - lead_rows
    total_sum = jnp.zeros((signal_in.shape[0], row_count, signal_in.shape[2]), jnp.float32)
    for offset in range(tap_weights.shape[1]):
        total_sum = total_sum + tap_weights[:, offset][:, None, :] * signal_in[:, lead_rows - offset:lead_rows - offset + row_count, :]
    return total_sum


def reference(projected, short_weight, filter_taps, out_weight):
    lead_rows = SHORT - 1
    padded = jnp.pad(projected.astype(jnp.float32), ((0, 0), (lead_rows, 0), (0, 0)))
    filtered = short_filter(padded, short_weight, lead_rows)
    query_part = filtered[0]
    mixed_input = (filtered[1] * filtered[2]).astype(jnp.bfloat16)
    length_full = 2 * TOKENS
    group_width = D // N_TP
    total_out = jnp.zeros((TOKENS, D), jnp.float32)
    for group_index in range(N_TP):
        lower = group_index * group_width
        signal = mixed_input[:, lower:lower + group_width].astype(jnp.float32)
        kernel = filter_taps[:, lower:lower + group_width]
        spectrum = jnp.fft.rfft(signal, n=length_full, axis=0) * jnp.fft.rfft(kernel, n=length_full, axis=0)
        long_output = jnp.fft.irfft(spectrum, n=length_full, axis=0)[:TOKENS].astype(jnp.bfloat16)
        long_output = lax.optimization_barrier(long_output)
        gated_rows = (query_part[:, lower:lower + group_width] * long_output.astype(jnp.float32)).astype(jnp.bfloat16)
        partial_out = jnp.dot(gated_rows, out_weight[lower:lower + group_width, :], preferred_element_type=jnp.float32)
        rounded = lax.optimization_barrier(partial_out.astype(jnp.bfloat16))
        total_out = total_out + rounded.astype(jnp.float32)
    return total_out.astype(jnp.bfloat16)
```

```python
import functools

import jax
import jax.numpy as jnp
import ml_dtypes
import numpy as np
from jax import lax
from jax.experimental import pallas as pl
from jax.experimental.pallas import tpu as pltpu
from jax.sharding import Mesh, PartitionSpec as P

F32, BF16 = jnp.float32, jnp.bfloat16
CTX = ("yl", "z", "c")
BLOCKS = 32
CH = 16
WIDE = 256
TOKENS = BLOCKS * WIDE
MIB = 1024 * 1024
VMEM = pl.BlockSpec(memory_space=pltpu.VMEM)
ANY = pl.BlockSpec(memory_space=pl.ANY)
SMEM = pl.BlockSpec(memory_space=pltpu.SMEM)


def call(kernel, out_shape, n_scalar, n_in, scratch=(), n_dep=0, vmem=56, flops=1000):
    return pl.pallas_call(
        kernel,
        out_shape=out_shape,
        in_specs=[ANY] * n_dep + [SMEM] * n_scalar + [VMEM] * n_in,
        out_specs=jax.tree.map(lambda _: VMEM, out_shape),
        scratch_shapes=list(scratch),
        compiler_params=pltpu.CompilerParams(vmem_limit_bytes=vmem * MIB),
        cost_estimate=pl.CostEstimate(flops=flops, bytes_accessed=1000, transcendentals=0),
    )


def table16(table):
    return table.astype(ml_dtypes.bfloat16)


@functools.lru_cache(None)
def tables():
    turn = 2.0 * np.pi
    eye = np.eye(CH)
    k1 = np.arange(BLOCKS) + 0.25
    n1 = np.arange(BLOCKS)
    outer = turn * np.outer(k1, n1) / BLOCKS
    first = np.concatenate([np.cos(outer), -np.sin(outer)], 0)
    first = np.kron(first, eye)
    last = np.concatenate([np.cos(outer.T), -np.sin(outer.T)], 1) / TOKENS
    last = np.kron(last, eye)
    n2 = np.arange(WIDE)
    twist = (turn * np.outer(k1, n2) / TOKENS)[:, None, :]
    inner = turn * (np.outer(n2, n2) % WIDE) / WIDE
    c, s = np.cos(inner), np.sin(inner)
    forward = np.block([[c, -s], [s, c]])
    backward = np.block([[c, s], [-s, c]])
    return dict(
        first=table16(first),
        last=table16(last),
        forward=table16(forward),
        backward=table16(backward),
        twist=(np.cos(twist).astype(np.float32), np.sin(twist).astype(np.float32)),
    )


def dot(a, b):
    return jnp.dot(a, b, preferred_element_type=F32)


def turn(re, im, cos, sin):
    shape = (BLOCKS, CH, WIDE)
    re, im = re.reshape(shape), im.reshape(shape)
    flat = (BLOCKS * CH, WIDE)
    return (re * cos + im * sin).reshape(flat), (im * cos - re * sin).reshape(flat)


def featurize_kernel(projected, lead, weight, mixed, query, padded):
    def filtered(m):
        padded[0:8, :] = jnp.zeros((8, padded.shape[1]), F32)
        padded[6:8, :] = lead[m].astype(F32)
        padded[8:, :] = projected[m].astype(F32)
        rows = projected.shape[1]
        total = weight[m, 0:1, :] * padded[8 : 8 + rows, :]
        total = total + weight[m, 1:2, :] * padded[7 : 7 + rows, :]
        return total + weight[m, 2:3, :] * padded[6 : 6 + rows, :]

    product = filtered(1) * filtered(2)
    mixed[...] = product.T.astype(BF16).reshape(mixed.shape)
    query[...] = filtered(0).T


def filter_kernel(taps, first, cos, sin, fwd, spectrum):
    rows = BLOCKS * CH
    outer = dot(first[...], taps[...].reshape(rows, WIDE).astype(BF16))
    turned = turn(outer[:rows], outer[rows:], cos[...], sin[...])
    spectrum[...] = dot(jnp.concatenate(turned, 1).astype(BF16), fwd[...])


def conv_kernel(dep, signal, spectrum, first, cos, sin, fwd, bwd, last, out):
    del dep
    rows = BLOCKS * CH
    outer = dot(first[...], signal[...].reshape(rows, WIDE))
    turned = turn(outer[:rows], outer[rows:], cos[...], sin[...])
    spec = dot(jnp.concatenate(turned, 1).astype(BF16), fwd[...])
    sr, si = spec[:, :WIDE], spec[:, WIDE:]
    hr, hi = spectrum[:, :WIDE], spectrum[:, WIDE:]
    both = jnp.concatenate([sr * hr - si * hi, sr * hi + si * hr], 1).astype(BF16)
    mid = dot(both, bwd[...])
    turned = turn(mid[:, :WIDE], mid[:, WIDE:], cos[...], -sin[...])
    out[...] = dot(last[...], jnp.concatenate(turned, 0).astype(BF16)).astype(BF16).reshape(out.shape)


def gate_kernel(dep, convolved, query, gated):
    del dep
    rows = (query[...] * convolved[...].reshape(query.shape).astype(F32)).T.astype(BF16)
    for copy in range(gated.shape[0]):
        gated[copy] = rows


def pair_kernel(signal, spectrum, own, mate, out):
    del signal, spectrum
    out[0] = own[...]
    out[1] = mate[...]


def quad_kernel(dep, own, other, out):
    del dep
    out[:, :, :WIDE] = own[...]
    out[:, :, WIDE:] = other[...]


def project_kernel(place, g_own, g_other, w0, w1, w2, w3, w4, keep, send, total):
    yl, z, core = place[0], place[1], place[2]
    total[...] = jnp.zeros_like(total)

    def add(step, row, block):
        source = (z + 8 + step * (2 * core - 1)) % 8
        group = 2 * row + source // 4
        total[group, 0] += dot(g_own[source % 4], block)
        total[group, 1] += dot(g_other[source % 4], block)

    mine = lax.rem(yl + core, 2)
    add(0, mine, w0[core])
    for step, ref in ((1, w1), (2, w2), (3, w3)):
        add(step, yl, ref[0])
        add(step, 1 - yl, ref[1])
    add(4, mine, w4[...])

    own = pl.ds(pl.multiple_of(core * WIDE, WIDE), WIDE)
    other = pl.ds(pl.multiple_of((1 - core) * WIDE, WIDE), WIDE)
    for group in range(4):
        for tokens, ref in ((0, keep), (1, send)):
            ref[group, :, own] = total[group, tokens, :, :WIDE].astype(BF16)
            ref[group, :, other] = total[group, tokens, :, WIDE:].astype(BF16)


def ring(n, shift):
    return [(i, (i + shift) % n) for i in range(n)]


def swap_pairs():
    def index(h, w, yh):
        return (4 * h + w) * 4 + yh

    return [(index(h, w, yh), index(h, yh, w)) for h in range(2) for w in range(4) for yh in range(4)]


def along(a):
    pairs = [((z * 2 + c), ((z + 1 - 2 * c) % 8) * 2 + c) for z in range(8) for c in range(2)]
    return lax.ppermute(a, ("z", "c"), pairs)


def tie(dep, *arrays, flops=1000):
    n = len(arrays)
    return pl.pallas_call(
        lambda *refs: None,
        out_shape=[jax.ShapeDtypeStruct(a.shape, a.dtype) for a in arrays],
        in_specs=[ANY] * (n + 1),
        out_specs=[ANY] * n,
        input_output_aliases={i + 1: i for i in range(n)},
        cost_estimate=pl.CostEstimate(flops=flops, bytes_accessed=1000, transcendentals=0),
    )(dep, *arrays)


def shards(projected, short_weight, filter_taps, out_weight):
    t = tables()
    width = projected.shape[2]
    rows = projected.shape[1]
    core = lax.axis_index("c")
    place = jnp.stack([lax.axis_index("yl"), lax.axis_index("z"), core]).astype(jnp.int32)

    order = [(i, i + 1) for i in range(BLOCKS - 1)]
    lead = lax.ppermute(projected[:, -2:], CTX, order)
    block = lax.ppermute(out_weight, ("z", "yh"), swap_pairs())

    mixed, query = call(
        featurize_kernel,
        [jax.ShapeDtypeStruct((BLOCKS, CH, WIDE), BF16), jax.ShapeDtypeStruct((width, rows), F32)],
        0, 3,
        [pltpu.VMEM((rows + 8, width), F32)],
    )(projected, lead, short_weight)
    signal = lax.all_to_all(mixed, CTX, split_axis=0, concat_axis=0, tiled=True)

    taps = filter_taps.T.reshape(CH, BLOCKS, WIDE).transpose(1, 0, 2)
    taps, = tie(mixed, taps)
    block, = tie(mixed, block)
    mate = lax.ppermute(block, "yl", ring(2, 1))
    spectrum = call(
        filter_kernel, jax.ShapeDtypeStruct((BLOCKS * CH, 2 * WIDE), F32), 0, 5
    )(taps, t["first"], *t["twist"], t["forward"])

    pair = call(pair_kernel, jax.ShapeDtypeStruct((2, width, WIDE), BF16), 0, 2, n_dep=2)(
        signal, spectrum, block, mate
    )
    other = lax.ppermute(pair, "c", ring(2, 1))
    convolved = call(
        conv_kernel, jax.ShapeDtypeStruct((BLOCKS, CH, WIDE), BF16), 0, 8, n_dep=1
    )(pair, signal, spectrum, t["first"], *t["twist"], t["forward"], t["backward"], t["last"])
    w0 = call(quad_kernel, jax.ShapeDtypeStruct((2, width, 2 * WIDE), BF16), 0, 2, n_dep=1)(
        convolved, pair, other
    )
    w1 = along(w0)
    convolved, = tie(w0, convolved)
    convolved = lax.all_to_all(convolved, CTX, split_axis=0, concat_axis=0, tiled=True)

    w1, = tie(convolved, w1)
    w2 = along(w1)
    gated = call(
        gate_kernel, jax.ShapeDtypeStruct((4, rows, width), BF16), 0, 2, n_dep=1
    )(w1, convolved, query)
    w2, = tie(gated, w2)
    w3 = along(w2)
    half = lax.dynamic_index_in_dim(w3, core, 0, keepdims=False)
    w4, = tie(half, along(half), flops=10**9)

    g_own = lax.all_to_all(gated, "yh", split_axis=0, concat_axis=0, tiled=True)
    g_own, = tie(half, g_own)
    g_other = lax.ppermute(g_own, "c", ring(2, 1))

    keep, send = call(
        project_kernel,
        [jax.ShapeDtypeStruct((4, rows, width), BF16)] * 2,
        1, 7,
        [pltpu.VMEM((4, 2, rows, width), F32)],
        vmem=24,
    )(place, g_own, g_other, w0, w1, w2, w3, w4)
    partial = (keep.astype(F32) + lax.ppermute(send, "c", ring(2, 1)).astype(F32)).astype(BF16)
    parts = lax.all_to_all(partial, "x", split_axis=0, concat_axis=0, tiled=True)
    return jnp.sum(parts.astype(F32), 0).astype(BF16)


def solution(mesh):
    fine = Mesh(mesh.devices.reshape(2, 8, 2, 4, 4), ("yl", "z", "c", "x", "yh"))
    tp = ("x", "yh")
    in_specs = (P(None, CTX, tp), P(None, None, tp), P(None, tp + CTX), P(tp, CTX))
    out_specs = P(CTX, tp)
    return jax.shard_map(shards, mesh=fine, in_specs=in_specs, out_specs=out_specs, check_vma=False)
```

```python
import functools

import jax
import jax.numpy as jnp
import ml_dtypes
import numpy as np
from jax import lax
from jax.experimental import pallas as pl
from jax.experimental.pallas import tpu as pltpu
from jax.sharding import Mesh, PartitionSpec as P

F32, BF16 = jnp.float32, jnp.bfloat16
CTX = ("yl", "z", "c")
BLOCKS = 32
CH = 16
WIDE = 256
TOKENS = BLOCKS * WIDE
MIB = 1024 * 1024
VMEM = pl.BlockSpec(memory_space=pltpu.VMEM)
ANY = pl.BlockSpec(memory_space=pl.ANY)
SMEM = pl.BlockSpec(memory_space=pltpu.SMEM)


def call(kernel, out_shape, n_scalar, n_in, scratch=(), n_dep=0, vmem=56, flops=1000):
    return pl.pallas_call(
        kernel,
        out_shape=out_shape,
        in_specs=[ANY] * n_dep + [SMEM] * n_scalar + [VMEM] * n_in,
        out_specs=jax.tree.map(lambda _: VMEM, out_shape),
        scratch_shapes=list(scratch),
        compiler_params=pltpu.CompilerParams(vmem_limit_bytes=vmem * MIB),
        cost_estimate=pl.CostEstimate(flops=flops, bytes_accessed=1000, transcendentals=0),
    )


def table16(table):
    return table.astype(ml_dtypes.bfloat16)


@functools.lru_cache(None)
def tables():
    turn = 2.0 * np.pi
    eye = np.eye(CH)
    k1 = np.arange(BLOCKS) + 0.25
    n1 = np.arange(BLOCKS)
    outer = turn * np.outer(k1, n1) / BLOCKS
    first = np.concatenate([np.cos(outer), -np.sin(outer)], 0)
    first = np.kron(first, eye)
    last = np.concatenate([np.cos(outer.T), -np.sin(outer.T)], 1) / TOKENS
    last = np.kron(last, eye)
    n2 = np.arange(WIDE)
    twist = (turn * np.outer(k1, n2) / TOKENS)[:, None, :]
    inner = turn * (np.outer(n2, n2) % WIDE) / WIDE
    c, s = np.cos(inner), np.sin(inner)
    forward = np.block([[c, -s], [s, c]])
    backward = np.block([[c, s], [-s, c]])
    return dict(
        first=table16(first),
        last=table16(last),
        forward=table16(forward),
        backward=table16(backward),
        twist=(np.cos(twist).astype(np.float32), np.sin(twist).astype(np.float32)),
    )


def dot(a, b):
    return jnp.dot(a, b, preferred_element_type=F32)


def turn(re, im, cos, sin):
    shape = (BLOCKS, CH, WIDE)
    re, im = re.reshape(shape), im.reshape(shape)
    flat = (BLOCKS * CH, WIDE)
    return (re * cos + im * sin).reshape(flat), (im * cos - re * sin).reshape(flat)


def featurize_kernel(projected, lead, weight, mixed, query, padded):
    def filtered(m):
        padded[0:8, :] = jnp.zeros((8, padded.shape[1]), F32)
        padded[6:8, :] = lead[m].astype(F32)
        padded[8:, :] = projected[m].astype(F32)
        rows = projected.shape[1]
        total = weight[m, 0:1, :] * padded[8 : 8 + rows, :]
        total = total + weight[m, 1:2, :] * padded[7 : 7 + rows, :]
        return total + weight[m, 2:3, :] * padded[6 : 6 + rows, :]

    product = filtered(1) * filtered(2)
    mixed[...] = product.T.astype(BF16).reshape(mixed.shape)
    query[...] = filtered(0).T


def filter_kernel(taps, first, cos, sin, fwd, spectrum):
    rows = BLOCKS * CH
    outer = dot(first[...], taps[...].reshape(rows, WIDE).astype(BF16))
    turned = turn(outer[:rows], outer[rows:], cos[...], sin[...])
    spectrum[...] = dot(jnp.concatenate(turned, 1).astype(BF16), fwd[...])


def conv_kernel(dep, signal, spectrum, first, cos, sin, fwd, bwd, last, out):
    del dep
    rows = BLOCKS * CH
    outer = dot(first[...], signal[...].reshape(rows, WIDE))
    turned = turn(outer[:rows], outer[rows:], cos[...], sin[...])
    spec = dot(jnp.concatenate(turned, 1).astype(BF16), fwd[...])
    sr, si = spec[:, :WIDE], spec[:, WIDE:]
    hr, hi = spectrum[:, :WIDE], spectrum[:, WIDE:]
    both = jnp.concatenate([sr * hr - si * hi, sr * hi + si * hr], 1).astype(BF16)
    mid = dot(both, bwd[...])
    turned = turn(mid[:, :WIDE], mid[:, WIDE:], cos[...], -sin[...])
    out[...] = dot(last[...], jnp.concatenate(turned, 0).astype(BF16)).astype(BF16).reshape(out.shape)


def gate_kernel(convolved, query, gated):
    rows = (query[...] * convolved[...].reshape(query.shape).astype(F32)).T.astype(BF16)
    for copy in range(gated.shape[0]):
        gated[copy] = rows


def pair_kernel(signal, spectrum, own, mate, out):
    del signal, spectrum
    out[0] = own[...]
    out[1] = mate[...]


def quad_kernel(dep, own, other, out):
    del dep
    out[:, :, :WIDE] = own[...]
    out[:, :, WIDE:] = other[...]


def project_kernel(place, g_own, g_other, w0, w1, w2, w3, w4, keep, send, total):
    yl, z, core = place[0], place[1], place[2]
    total[...] = jnp.zeros_like(total)

    def add(step, row, block):
        source = (z + 8 + step * (2 * core - 1)) % 8
        group = 2 * row + source // 4
        total[group, 0] += dot(g_own[source % 4], block)
        total[group, 1] += dot(g_other[source % 4], block)

    mine = lax.rem(yl + core, 2)
    add(0, mine, w0[core])
    for step, ref in ((1, w1), (2, w2), (3, w3)):
        add(step, yl, ref[0])
        add(step, 1 - yl, ref[1])
    add(4, mine, w4[...])

    own = pl.ds(pl.multiple_of(core * WIDE, WIDE), WIDE)
    other = pl.ds(pl.multiple_of((1 - core) * WIDE, WIDE), WIDE)
    for group in range(4):
        for tokens, ref in ((0, keep), (1, send)):
            ref[group, :, own] = total[group, tokens, :, :WIDE].astype(BF16)
            ref[group, :, other] = total[group, tokens, :, WIDE:].astype(BF16)


def ring(n, shift):
    return [(i, (i + shift) % n) for i in range(n)]


def swap_pairs():
    def index(h, w, yh):
        return (4 * h + w) * 4 + yh

    return [(index(h, w, yh), index(h, yh, w)) for h in range(2) for w in range(4) for yh in range(4)]


def along(a):
    pairs = [((z * 2 + c), ((z + 1 - 2 * c) % 8) * 2 + c) for z in range(8) for c in range(2)]
    return lax.ppermute(a, ("z", "c"), pairs)


def tie(dep, *arrays, flops=1000):
    n = len(arrays)
    return pl.pallas_call(
        lambda *refs: None,
        out_shape=[jax.ShapeDtypeStruct(a.shape, a.dtype) for a in arrays],
        in_specs=[ANY] * (n + 1),
        out_specs=[ANY] * n,
        input_output_aliases={i + 1: i for i in range(n)},
        cost_estimate=pl.CostEstimate(flops=flops, bytes_accessed=1000, transcendentals=0),
    )(dep, *arrays)


def shards(projected, short_weight, filter_taps, out_weight):
    t = tables()
    width = projected.shape[2]
    rows = projected.shape[1]
    core = lax.axis_index("c")
    place = jnp.stack([lax.axis_index("yl"), lax.axis_index("z"), core]).astype(jnp.int32)

    order = [(i, i + 1) for i in range(BLOCKS - 1)]
    lead = lax.ppermute(projected[:, -2:], CTX, order)
    block = lax.ppermute(out_weight, ("z", "yh"), swap_pairs())

    mixed, query = call(
        featurize_kernel,
        [jax.ShapeDtypeStruct((BLOCKS, CH, WIDE), BF16), jax.ShapeDtypeStruct((width, rows), F32)],
        0, 3,
        [pltpu.VMEM((rows + 8, width), F32)],
    )(projected, lead, short_weight)
    signal = lax.all_to_all(mixed, CTX, split_axis=0, concat_axis=0, tiled=True)

    taps = filter_taps.T.reshape(CH, BLOCKS, WIDE).transpose(1, 0, 2)
    taps, = tie(mixed, taps)
    block, = tie(mixed, block)
    mate = lax.ppermute(block, "yl", ring(2, 1))
    spectrum = call(
        filter_kernel, jax.ShapeDtypeStruct((BLOCKS * CH, 2 * WIDE), F32), 0, 5
    )(taps, t["first"], *t["twist"], t["forward"])

    pair = call(pair_kernel, jax.ShapeDtypeStruct((2, width, WIDE), BF16), 0, 2, n_dep=2)(
        signal, spectrum, block, mate
    )
    other = lax.ppermute(pair, "c", ring(2, 1))
    convolved = call(
        conv_kernel, jax.ShapeDtypeStruct((BLOCKS, CH, WIDE), BF16), 0, 8, n_dep=1
    )(pair, signal, spectrum, t["first"], *t["twist"], t["forward"], t["backward"], t["last"])
    w0 = call(quad_kernel, jax.ShapeDtypeStruct((2, width, 2 * WIDE), BF16), 0, 2, n_dep=1)(
        convolved, pair, other
    )
    w1 = along(w0)
    convolved, = tie(w0, convolved)
    w1, = tie(convolved, w1)
    convolved = lax.all_to_all(convolved, CTX, split_axis=0, concat_axis=0, tiled=True)
    w2 = along(w1)
    gated = call(
        gate_kernel, jax.ShapeDtypeStruct((4, rows, width), BF16), 0, 2, flops=6 * 10**9
    )(convolved, query)
    w2, = tie(gated, w2)
    w3 = along(w2)
    half = lax.dynamic_index_in_dim(w3, core, 0, keepdims=False)
    w4, = tie(half, along(half), flops=10**10)

    g_own = lax.all_to_all(gated, "yh", split_axis=0, concat_axis=0, tiled=True)
    g_own, = tie(half, g_own, flops=10**10)
    g_other = lax.ppermute(g_own, "c", ring(2, 1))

    keep, send = call(
        project_kernel,
        [jax.ShapeDtypeStruct((4, rows, width), BF16)] * 2,
        1, 7,
        [pltpu.VMEM((4, 2, rows, width), F32)],
        vmem=24,
    )(place, g_own, g_other, w0, w1, w2, w3, w4)
    partial = (keep.astype(F32) + lax.ppermute(send, "c", ring(2, 1)).astype(F32)).astype(BF16)
    parts = lax.all_to_all(partial, "x", split_axis=0, concat_axis=0, tiled=True)
    return jnp.sum(parts.astype(F32), 0).astype(BF16)


def solution(mesh):
    fine = Mesh(mesh.devices.reshape(2, 8, 2, 4, 4), ("yl", "z", "c", "x", "yh"))
    tp = ("x", "yh")
    in_specs = (P(None, CTX, tp), P(None, None, tp), P(None, tp + CTX), P(tp, CTX))
    out_specs = P(CTX, tp)
    return jax.shard_map(shards, mesh=fine, in_specs=in_specs, out_specs=out_specs, check_vma=False)
```

```python
import functools

import jax
import jax.numpy as jnp
import ml_dtypes
import numpy as np
from jax import lax
from jax.experimental import pallas as pl
from jax.experimental.pallas import tpu as pltpu
from jax.sharding import Mesh, PartitionSpec as P

F32, BF16 = jnp.float32, jnp.bfloat16
CTX = ("yl", "z", "c")
BLOCKS = 32
CH = 16
WIDE = 256
TOKENS = BLOCKS * WIDE
MIB = 1024 * 1024
VMEM = pl.BlockSpec(memory_space=pltpu.VMEM)
ANY = pl.BlockSpec(memory_space=pl.ANY)
SMEM = pl.BlockSpec(memory_space=pltpu.SMEM)


def call(kernel, out_shape, n_scalar, n_in, scratch=(), n_dep=0, vmem=56, flops=1000):
    return pl.pallas_call(
        kernel,
        out_shape=out_shape,
        in_specs=[ANY] * n_dep + [SMEM] * n_scalar + [VMEM] * n_in,
        out_specs=jax.tree.map(lambda _: VMEM, out_shape),
        scratch_shapes=list(scratch),
        compiler_params=pltpu.CompilerParams(vmem_limit_bytes=vmem * MIB),
        cost_estimate=pl.CostEstimate(flops=flops, bytes_accessed=1000, transcendentals=0),
    )


def table16(table):
    return table.astype(ml_dtypes.bfloat16)


@functools.lru_cache(None)
def tables():
    turn = 2.0 * np.pi
    eye = np.eye(CH)
    k1 = np.arange(BLOCKS) + 0.25
    n1 = np.arange(BLOCKS)
    outer = turn * np.outer(k1, n1) / BLOCKS
    first = np.concatenate([np.cos(outer), -np.sin(outer)], 0)
    first = np.kron(first, eye)
    last = np.concatenate([np.cos(outer.T), -np.sin(outer.T)], 1) / TOKENS
    last = np.kron(last, eye)
    n2 = np.arange(WIDE)
    twist = (turn * np.outer(k1, n2) / TOKENS)[:, None, :]
    inner = turn * (np.outer(n2, n2) % WIDE) / WIDE
    c, s = np.cos(inner), np.sin(inner)
    forward = np.block([[c, -s], [s, c]])
    backward = np.block([[c, s], [-s, c]])
    return dict(
        first=table16(first),
        last=table16(last),
        forward=table16(forward),
        backward=table16(backward),
        twist=(np.cos(twist).astype(np.float32), np.sin(twist).astype(np.float32)),
    )


def dot(a, b):
    return jnp.dot(a, b, preferred_element_type=F32)


def turn(re, im, cos, sin):
    shape = (BLOCKS, CH, WIDE)
    re, im = re.reshape(shape), im.reshape(shape)
    flat = (BLOCKS * CH, WIDE)
    return (re * cos + im * sin).reshape(flat), (im * cos - re * sin).reshape(flat)


def featurize_kernel(projected, lead, weight, mixed, query, padded):
    def filtered(m):
        padded[0:8, :] = jnp.zeros((8, padded.shape[1]), F32)
        padded[6:8, :] = lead[m].astype(F32)
        padded[8:, :] = projected[m].astype(F32)
        rows = projected.shape[1]
        total = weight[m, 0:1, :] * padded[8 : 8 + rows, :]
        total = total + weight[m, 1:2, :] * padded[7 : 7 + rows, :]
        return total + weight[m, 2:3, :] * padded[6 : 6 + rows, :]

    product = filtered(1) * filtered(2)
    mixed[...] = product.T.astype(BF16).reshape(mixed.shape)
    query[...] = filtered(0).T


def filter_kernel(taps, first, cos, sin, fwd, spectrum):
    rows = BLOCKS * CH
    outer = dot(first[...], taps[...].reshape(rows, WIDE).astype(BF16))
    turned = turn(outer[:rows], outer[rows:], cos[...], sin[...])
    spectrum[...] = dot(jnp.concatenate(turned, 1).astype(BF16), fwd[...])


def conv_kernel(dep, signal, spectrum, first, cos, sin, fwd, bwd, last, out):
    del dep
    rows = BLOCKS * CH
    outer = dot(first[...], signal[...].reshape(rows, WIDE))
    turned = turn(outer[:rows], outer[rows:], cos[...], sin[...])
    spec = dot(jnp.concatenate(turned, 1).astype(BF16), fwd[...])
    sr, si = spec[:, :WIDE], spec[:, WIDE:]
    hr, hi = spectrum[:, :WIDE], spectrum[:, WIDE:]
    both = jnp.concatenate([sr * hr - si * hi, sr * hi + si * hr], 1).astype(BF16)
    mid = dot(both, bwd[...])
    turned = turn(mid[:, :WIDE], mid[:, WIDE:], cos[...], -sin[...])
    out[...] = dot(last[...], jnp.concatenate(turned, 0).astype(BF16)).astype(BF16).reshape(out.shape)


def gate_kernel(convolved, query, gated):
    rows = (query[...] * convolved[...].reshape(query.shape).astype(F32)).T.astype(BF16)
    for copy in range(gated.shape[0]):
        gated[copy] = rows


def pair_kernel(signal, spectrum, own, mate, out):
    del signal, spectrum
    out[0] = own[...]
    out[1] = mate[...]


def quad_kernel(dep, own, other, out):
    del dep
    out[:, :, :WIDE] = own[...]
    out[:, :, WIDE:] = other[...]


def project_kernel(
    place, g_own, other_ref, w0, w1_ref, w2, w3_ref, w4_ref, keep, send, g_other, w1, w3, w4, total, sems
):
    yl, z, core = place[0], place[1], place[2]
    mine = lax.rem(yl + core, 2)
    pairs = ((w1_ref, w1), (w3_ref, w3), (other_ref, g_other), (w4_ref, w4))
    copies = [pltpu.make_async_copy(a, b, sems.at[i]) for i, (a, b) in enumerate(pairs)]
    for copy in copies:
        copy.start()
    total[...] = jnp.zeros_like(total)

    def add(tokens, step, row, block):
        source = (z + 8 + step * (2 * core - 1)) % 8
        rows = g_other if tokens else g_own
        total[2 * row + source // 4, tokens] += dot(rows[source % 4], block)

    def both(tokens, step, ref):
        add(tokens, step, yl, ref[0])
        add(tokens, step, 1 - yl, ref[1])

    add(0, 0, mine, w0[core])
    both(0, 2, w2)
    copies[0].wait()
    both(0, 1, w1)
    copies[1].wait()
    both(0, 3, w3)
    copies[2].wait()
    add(1, 0, mine, w0[core])
    for step, ref in ((1, w1), (2, w2), (3, w3)):
        both(1, step, ref)
    copies[3].wait()
    for tokens in range(2):
        add(tokens, 4, mine, w4[...])

    own = pl.ds(pl.multiple_of(core * WIDE, WIDE), WIDE)
    other = pl.ds(pl.multiple_of((1 - core) * WIDE, WIDE), WIDE)
    for group in range(4):
        for tokens, ref in ((0, keep), (1, send)):
            ref[group, :, own] = total[group, tokens, :, :WIDE].astype(BF16)
            ref[group, :, other] = total[group, tokens, :, WIDE:].astype(BF16)


def ring(n, shift):
    return [(i, (i + shift) % n) for i in range(n)]


def swap_pairs():
    def index(h, w, yh):
        return (4 * h + w) * 4 + yh

    return [(index(h, w, yh), index(h, yh, w)) for h in range(2) for w in range(4) for yh in range(4)]


def along(a):
    pairs = [((z * 2 + c), ((z + 1 - 2 * c) % 8) * 2 + c) for z in range(8) for c in range(2)]
    return lax.ppermute(a, ("z", "c"), pairs)


def tie(dep, *arrays, flops=1000):
    n = len(arrays)
    return pl.pallas_call(
        lambda *refs: None,
        out_shape=[jax.ShapeDtypeStruct(a.shape, a.dtype) for a in arrays],
        in_specs=[ANY] * (n + 1),
        out_specs=[ANY] * n,
        input_output_aliases={i + 1: i for i in range(n)},
        cost_estimate=pl.CostEstimate(flops=flops, bytes_accessed=1000, transcendentals=0),
    )(dep, *arrays)


def shards(projected, short_weight, filter_taps, out_weight):
    t = tables()
    width = projected.shape[2]
    rows = projected.shape[1]
    core = lax.axis_index("c")
    place = jnp.stack([lax.axis_index("yl"), lax.axis_index("z"), core]).astype(jnp.int32)

    order = [(i, i + 1) for i in range(BLOCKS - 1)]
    lead = lax.ppermute(projected[:, -2:], CTX, order)
    block = lax.ppermute(out_weight, ("z", "yh"), swap_pairs())

    mixed, query = call(
        featurize_kernel,
        [jax.ShapeDtypeStruct((BLOCKS, CH, WIDE), BF16), jax.ShapeDtypeStruct((width, rows), F32)],
        0, 3,
        [pltpu.VMEM((rows + 8, width), F32)],
    )(projected, lead, short_weight)
    signal = lax.all_to_all(mixed, CTX, split_axis=0, concat_axis=0, tiled=True)

    taps = filter_taps.T.reshape(CH, BLOCKS, WIDE).transpose(1, 0, 2)
    taps, = tie(mixed, taps)
    block, = tie(mixed, block)
    mate = lax.ppermute(block, "yl", ring(2, 1))
    spectrum = call(
        filter_kernel, jax.ShapeDtypeStruct((BLOCKS * CH, 2 * WIDE), F32), 0, 5
    )(taps, t["first"], *t["twist"], t["forward"])

    pair = call(pair_kernel, jax.ShapeDtypeStruct((2, width, WIDE), BF16), 0, 2, n_dep=2)(
        signal, spectrum, block, mate
    )
    other = lax.ppermute(pair, "c", ring(2, 1))
    convolved = call(
        conv_kernel, jax.ShapeDtypeStruct((BLOCKS, CH, WIDE), BF16), 0, 8, n_dep=1
    )(pair, signal, spectrum, t["first"], *t["twist"], t["forward"], t["backward"], t["last"])
    w0 = call(quad_kernel, jax.ShapeDtypeStruct((2, width, 2 * WIDE), BF16), 0, 2, n_dep=1)(
        convolved, pair, other
    )
    w1 = along(w0)
    convolved, = tie(w0, convolved)
    convolved = lax.all_to_all(convolved, CTX, split_axis=0, concat_axis=0, tiled=True)
    w2 = along(w1)
    gated = call(
        gate_kernel, jax.ShapeDtypeStruct((4, rows, width), BF16), 0, 2, flops=6 * 10**9
    )(convolved, query)
    w3 = along(w2)
    half = lax.dynamic_index_in_dim(w3, core, 0, keepdims=False)
    w4, = tie(half, along(half), flops=10**10)

    g_own = lax.all_to_all(gated, "yh", split_axis=0, concat_axis=0, tiled=True)
    g_own, = tie(half, g_own, flops=10**10)
    g_other = lax.ppermute(g_own, "c", ring(2, 1))

    keep, send = pl.pallas_call(
        project_kernel,
        out_shape=[jax.ShapeDtypeStruct((4, rows, width), BF16)] * 2,
        in_specs=[SMEM, VMEM, ANY, VMEM, ANY, VMEM, ANY, ANY],
        out_specs=[VMEM] * 2,
        scratch_shapes=[
            pltpu.VMEM((4, rows, width), BF16),
            pltpu.VMEM((2, width, width), BF16),
            pltpu.VMEM((2, width, width), BF16),
            pltpu.VMEM((width, width), BF16),
            pltpu.VMEM((4, 2, rows, width), F32),
            pltpu.SemaphoreType.DMA((4,)),
        ],
        compiler_params=pltpu.CompilerParams(vmem_limit_bytes=24 * MIB),
        cost_estimate=pl.CostEstimate(flops=1000, bytes_accessed=1000, transcendentals=0),
    )(place, g_own, g_other, w0, w1, w2, w3, w4)
    partial = (keep.astype(F32) + lax.ppermute(send, "c", ring(2, 1)).astype(F32)).astype(BF16)
    parts = lax.all_to_all(partial, "x", split_axis=0, concat_axis=0, tiled=True)
    return jnp.sum(parts.astype(F32), 0).astype(BF16)


def solution(mesh):
    fine = Mesh(mesh.devices.reshape(2, 8, 2, 4, 4), ("yl", "z", "c", "x", "yh"))
    tp = ("x", "yh")
    in_specs = (P(None, CTX, tp), P(None, None, tp), P(None, tp + CTX), P(tp, CTX))
    out_specs = P(CTX, tp)
    return jax.shard_map(shards, mesh=fine, in_specs=in_specs, out_specs=out_specs, check_vma=False)
```

```python
import functools

import jax
import jax.numpy as jnp
import ml_dtypes
import numpy as np
from jax import lax
from jax.experimental import pallas as pl
from jax.experimental.pallas import tpu as pltpu
from jax.sharding import Mesh, PartitionSpec as P

F32, BF16 = jnp.float32, jnp.bfloat16
CTX = ("yl", "z", "c")
BLOCKS = 32
CH = 16
WIDE = 256
TOKENS = BLOCKS * WIDE
MIB = 1024 * 1024
VMEM = pl.BlockSpec(memory_space=pltpu.VMEM)
ANY = pl.BlockSpec(memory_space=pl.ANY)
SMEM = pl.BlockSpec(memory_space=pltpu.SMEM)


def call(kernel, out_shape, n_scalar, n_in, scratch=(), n_dep=0, vmem=56, flops=1000):
    return pl.pallas_call(
        kernel,
        out_shape=out_shape,
        in_specs=[ANY] * n_dep + [SMEM] * n_scalar + [VMEM] * n_in,
        out_specs=jax.tree.map(lambda _: VMEM, out_shape),
        scratch_shapes=list(scratch),
        compiler_params=pltpu.CompilerParams(vmem_limit_bytes=vmem * MIB),
        cost_estimate=pl.CostEstimate(flops=flops, bytes_accessed=1000, transcendentals=0),
    )


def table16(table):
    return table.astype(ml_dtypes.bfloat16)


@functools.lru_cache(None)
def tables():
    turn = 2.0 * np.pi
    eye = np.eye(CH)
    k1 = np.arange(BLOCKS) + 0.25
    n1 = np.arange(BLOCKS)
    outer = turn * np.outer(k1, n1) / BLOCKS
    first = np.concatenate([np.cos(outer), -np.sin(outer)], 0)
    first = np.kron(first, eye)
    last = np.concatenate([np.cos(outer.T), -np.sin(outer.T)], 1) / TOKENS
    last = np.kron(last, eye)
    n2 = np.arange(WIDE)
    twist = (turn * np.outer(k1, n2) / TOKENS)[:, None, :]
    inner = turn * (np.outer(n2, n2) % WIDE) / WIDE
    c, s = np.cos(inner), np.sin(inner)
    forward = np.block([[c, -s], [s, c]])
    backward = np.block([[c, s], [-s, c]])
    return dict(
        first=table16(first),
        last=table16(last),
        forward=table16(forward),
        backward=table16(backward),
        twist=(np.cos(twist).astype(np.float32), np.sin(twist).astype(np.float32)),
    )


def dot(a, b):
    return jnp.dot(a, b, preferred_element_type=F32)


def turn(re, im, cos, sin):
    shape = (BLOCKS, CH, WIDE)
    re, im = re.reshape(shape), im.reshape(shape)
    flat = (BLOCKS * CH, WIDE)
    return (re * cos + im * sin).reshape(flat), (im * cos - re * sin).reshape(flat)


def featurize_kernel(projected, lead, weight, mixed, query, padded):
    def filtered(m):
        padded[0:8, :] = jnp.zeros((8, padded.shape[1]), F32)
        padded[6:8, :] = lead[m].astype(F32)
        padded[8:, :] = projected[m].astype(F32)
        rows = projected.shape[1]
        total = weight[m, 0:1, :] * padded[8 : 8 + rows, :]
        total = total + weight[m, 1:2, :] * padded[7 : 7 + rows, :]
        return total + weight[m, 2:3, :] * padded[6 : 6 + rows, :]

    product = filtered(1) * filtered(2)
    mixed[...] = product.T.astype(BF16).reshape(mixed.shape)
    query[...] = filtered(0).T


def filter_kernel(taps, first, cos, sin, fwd, spectrum):
    rows = BLOCKS * CH
    outer = dot(first[...], taps[...].reshape(rows, WIDE).astype(BF16))
    turned = turn(outer[:rows], outer[rows:], cos[...], sin[...])
    spectrum[...] = dot(jnp.concatenate(turned, 1).astype(BF16), fwd[...])


def conv_kernel(dep, signal, spectrum, first, cos, sin, fwd, bwd, last, out):
    del dep
    rows = BLOCKS * CH
    outer = dot(first[...], signal[...].reshape(rows, WIDE))
    turned = turn(outer[:rows], outer[rows:], cos[...], sin[...])
    spec = dot(jnp.concatenate(turned, 1).astype(BF16), fwd[...])
    sr, si = spec[:, :WIDE], spec[:, WIDE:]
    hr, hi = spectrum[:, :WIDE], spectrum[:, WIDE:]
    both = jnp.concatenate([sr * hr - si * hi, sr * hi + si * hr], 1).astype(BF16)
    mid = dot(both, bwd[...])
    turned = turn(mid[:, :WIDE], mid[:, WIDE:], cos[...], -sin[...])
    out[...] = dot(last[...], jnp.concatenate(turned, 0).astype(BF16)).astype(BF16).reshape(out.shape)


def gate_kernel(convolved, query, gated):
    rows = (query[...] * convolved[...].reshape(query.shape).astype(F32)).T.astype(BF16)
    for copy in range(gated.shape[0]):
        gated[copy] = rows


def pair_kernel(signal, spectrum, own, mate, out):
    del signal, spectrum
    out[0] = own[...]
    out[1] = mate[...]


def quad_kernel(dep, own, other, out):
    del dep
    out[:, :, :WIDE] = own[...]
    out[:, :, WIDE:] = other[...]


def project_kernel(
    place, g_own, other_ref, w0, w1_ref, w2, w3_ref, w4_ref, keep, send, g_other, w1, w3, w4, total, sems
):
    yl, z, core = place[0], place[1], place[2]
    mine = lax.rem(yl + core, 2)
    pairs = ((w1_ref, w1), (w3_ref, w3), (other_ref, g_other), (w4_ref, w4))
    copies = [pltpu.make_async_copy(a, b, sems.at[i]) for i, (a, b) in enumerate(pairs)]
    for copy in copies:
        copy.start()
    total[...] = jnp.zeros_like(total)

    def add(tokens, step, row, block):
        source = (z + 8 + step * (2 * core - 1)) % 8
        rows = g_other if tokens else g_own
        total[2 * row + source // 4, tokens] += dot(rows[source % 4], block)

    def both(tokens, step, ref):
        add(tokens, step, yl, ref[0])
        add(tokens, step, 1 - yl, ref[1])

    add(0, 0, mine, w0[core])
    both(0, 2, w2)
    copies[0].wait()
    both(0, 1, w1)
    copies[1].wait()
    both(0, 3, w3)
    copies[2].wait()
    add(1, 0, mine, w0[core])
    for step, ref in ((1, w1), (2, w2), (3, w3)):
        both(1, step, ref)
    copies[3].wait()
    for tokens in range(2):
        add(tokens, 4, mine, w4[...])

    own = pl.ds(pl.multiple_of(core * WIDE, WIDE), WIDE)
    other = pl.ds(pl.multiple_of((1 - core) * WIDE, WIDE), WIDE)
    for group in range(4):
        for tokens, ref in ((0, keep), (1, send)):
            ref[group, :, own] = total[group, tokens, :, :WIDE].astype(BF16)
            ref[group, :, other] = total[group, tokens, :, WIDE:].astype(BF16)


def ring(n, shift):
    return [(i, (i + shift) % n) for i in range(n)]


def swap_pairs():
    def index(h, w, yh):
        return (4 * h + w) * 4 + yh

    return [(index(h, w, yh), index(h, yh, w)) for h in range(2) for w in range(4) for yh in range(4)]


def along(a):
    pairs = [((z * 2 + c), ((z + 1 - 2 * c) % 8) * 2 + c) for z in range(8) for c in range(2)]
    return lax.ppermute(a, ("z", "c"), pairs)


def tie(dep, *arrays, flops=1000):
    n = len(arrays)
    return pl.pallas_call(
        lambda *refs: None,
        out_shape=[jax.ShapeDtypeStruct(a.shape, a.dtype) for a in arrays],
        in_specs=[ANY] * (n + 1),
        out_specs=[ANY] * n,
        input_output_aliases={i + 1: i for i in range(n)},
        compiler_params=pltpu.CompilerParams(vmem_limit_bytes=MIB),
        cost_estimate=pl.CostEstimate(flops=flops, bytes_accessed=1000, transcendentals=0),
    )(dep, *arrays)


def shards(projected, short_weight, filter_taps, out_weight):
    t = tables()
    width = projected.shape[2]
    rows = projected.shape[1]
    core = lax.axis_index("c")
    place = jnp.stack([lax.axis_index("yl"), lax.axis_index("z"), core]).astype(jnp.int32)

    order = [(i, i + 1) for i in range(BLOCKS - 1)]
    lead = lax.ppermute(projected[:, -2:], CTX, order)
    block = lax.ppermute(out_weight, ("z", "yh"), swap_pairs())

    mixed, query = call(
        featurize_kernel,
        [jax.ShapeDtypeStruct((BLOCKS, CH, WIDE), BF16), jax.ShapeDtypeStruct((width, rows), F32)],
        0, 3,
        [pltpu.VMEM((rows + 8, width), F32)],
    )(projected, lead, short_weight)
    signal = lax.all_to_all(mixed, CTX, split_axis=0, concat_axis=0, tiled=True)

    taps = filter_taps.T.reshape(CH, BLOCKS, WIDE).transpose(1, 0, 2)
    taps, = tie(mixed, taps)
    block, = tie(mixed, block)
    mate = lax.ppermute(block, "yl", ring(2, 1))
    spectrum = call(
        filter_kernel, jax.ShapeDtypeStruct((BLOCKS * CH, 2 * WIDE), F32), 0, 5
    )(taps, t["first"], *t["twist"], t["forward"])

    pair = call(pair_kernel, jax.ShapeDtypeStruct((2, width, WIDE), BF16), 0, 2, n_dep=2)(
        signal, spectrum, block, mate
    )
    other = lax.ppermute(pair, "c", ring(2, 1))
    convolved = call(
        conv_kernel, jax.ShapeDtypeStruct((BLOCKS, CH, WIDE), BF16), 0, 8, n_dep=1
    )(pair, signal, spectrum, t["first"], *t["twist"], t["forward"], t["backward"], t["last"])
    w0 = call(quad_kernel, jax.ShapeDtypeStruct((2, width, 2 * WIDE), BF16), 0, 2, n_dep=1)(
        convolved, pair, other
    )
    w1 = along(w0)
    convolved, = tie(w0, convolved)
    convolved = lax.all_to_all(convolved, CTX, split_axis=0, concat_axis=0, tiled=True)
    w2 = along(w1)
    gated = call(
        gate_kernel, jax.ShapeDtypeStruct((4, rows, width), BF16), 0, 2, flops=6 * 10**9
    )(convolved, query)
    w3 = along(w2)
    half = lax.dynamic_index_in_dim(w3, core, 0, keepdims=False)
    w4, = tie(half, along(half), flops=10**10)

    g_own = lax.all_to_all(gated, "yh", split_axis=0, concat_axis=0, tiled=True)
    g_own, = tie(half, g_own, flops=10**10)
    g_other = lax.ppermute(g_own, "c", ring(2, 1))

    keep, send = pl.pallas_call(
        project_kernel,
        out_shape=[jax.ShapeDtypeStruct((4, rows, width), BF16)] * 2,
        in_specs=[SMEM, VMEM, ANY, VMEM, ANY, VMEM, ANY, ANY],
        out_specs=[VMEM] * 2,
        scratch_shapes=[
            pltpu.VMEM((4, rows, width), BF16),
            pltpu.VMEM((2, width, width), BF16),
            pltpu.VMEM((2, width, width), BF16),
            pltpu.VMEM((width, width), BF16),
            pltpu.VMEM((4, 2, rows, width), F32),
            pltpu.SemaphoreType.DMA((4,)),
        ],
        compiler_params=pltpu.CompilerParams(vmem_limit_bytes=24 * MIB),
        cost_estimate=pl.CostEstimate(flops=1000, bytes_accessed=1000, transcendentals=0),
    )(place, g_own, g_other, w0, w1, w2, w3, w4)
    partial = (keep.astype(F32) + lax.ppermute(send, "c", ring(2, 1)).astype(F32)).astype(BF16)
    parts = lax.all_to_all(partial, "x", split_axis=0, concat_axis=0, tiled=True)
    return jnp.sum(parts.astype(F32), 0).astype(BF16)


def solution(mesh):
    fine = Mesh(mesh.devices.reshape(2, 8, 2, 4, 4), ("yl", "z", "c", "x", "yh"))
    tp = ("x", "yh")
    in_specs = (P(None, CTX, tp), P(None, None, tp), P(None, tp + CTX), P(tp, CTX))
    out_specs = P(CTX, tp)
    return jax.shard_map(shards, mesh=fine, in_specs=in_specs, out_specs=out_specs, check_vma=False)
```
